32 devices in a mesh: row: 4 (over x, core), col: 8 (over z, y).
Axes of the slice: x: 2, y: 2, z: 4, core: 2. Of those that a mesh axis runs over, the one named last changes fastest.
Arguments:
- series: bfloat16 [512, 8192], P(None, ('row', 'col')), may hold values from -6 to 6
- lag_weight: float32 [4], replicated, may hold values from 0.25 to 1
- start_basis: bfloat16 [64, 8192], P(None, ('row', 'col')), may hold values from -5.25 to 5.25
- block_pairs: int32 [4, 8, 32, 2], P('row', 'col'), may hold values from 0 to 31, as said below
- pair_count: int32 [4, 8], P('row', 'col'), may hold values from 1 to 32, as said below
Outputs:
- basis: float32 [64, 8192], P(None, ('row', 'col'))
- rayleigh: float32 [64, 64], replicated
The draws below stay inside these ranges and needn't reach their ends.
Inputs may be any that keep to these rules, and one draw needn't show every extreme that they name: For every slot s of device (r, c), block_pairs[r, c, s, 0] is a block of row group r, from r * 8 to (r + 1) * 8 - 1, and block_pairs[r, c, s, 1] is a block held by a device of mesh column c: (block_pairs[r, c, s, 1]) mod (8) equals c. Slots that are not live hold blocks of the same ranges and are no part of the network. `pair_count`: the number of live slots of device (r, c); some device has exactly 32.
All inputs are finite; a program needn't handle non-finite values.
Results may differ from the reference program's by a relative error of at most 0.0045.
Values may be sent and summed in bfloat16 or wider, within the bound.
A program may use at most 64 MiB of HBM per device.

```python
import math
import jax
import jax.numpy as jnp
from jax import lax

BLOCK = 256
DAYS = 512
LAGS = 4
RANK = 64
ITERS = 2
BLK_DEV = 1
SLOTS = 32
CELLS = 8192
N_ROW = 4
N_COL = 8


def draw_block_pairs(key, part):
    lead_key = jax.random.fold_in(key, 11)
    trail_key = jax.random.fold_in(key, 13)
    within_key = jax.random.fold_in(key, 17)
    shape_all = (N_ROW, N_COL, SLOTS)
    row_groups = jnp.arange(N_ROW, dtype=jnp.int32).reshape(N_ROW, 1, 1)
    col_groups = jnp.arange(N_COL, dtype=jnp.int32).reshape(1, N_COL, 1)
    lead_ids = row_groups * (BLK_DEV * N_COL) + jax.random.randint(lead_key, shape_all, 0, BLK_DEV * N_COL)
    trail_rows = jax.random.randint(trail_key, shape_all, 0, N_ROW)
    trail_ids = (trail_rows * N_COL + col_groups) * BLK_DEV + jax.random.randint(within_key, shape_all, 0, BLK_DEV)
    return jnp.stack([lead_ids, trail_ids], axis=-1).astype(jnp.int32)


def draw_pair_count(key, part):
    first_key = jax.random.fold_in(key, 7)
    second_key = jax.random.fold_in(key, 9)
    chosen_key = jax.random.fold_in(key, 19)
    device_total = N_ROW * N_COL
    first_draw = jax.random.randint(first_key, (device_total,), 1, SLOTS + 1)
    second_draw = jax.random.randint(second_key, (device_total,), 1, SLOTS + 1)
    counts = jnp.maximum(1, first_draw * second_draw // SLOTS)
    chosen = jax.random.randint(chosen_key, (), 0, device_total)
    counts = jnp.where(jnp.arange(device_total) == chosen, SLOTS, counts)
    return counts.reshape(N_ROW, N_COL).astype(jnp.int32)


def draw_start_basis(key, part):
    sign_key = jax.random.fold_in(key, 23)
    strength_key = jax.random.fold_in(key, 29)
    shared_key = jax.random.fold_in(key, 31)
    own_key = jax.random.fold_in(key, 37)
    signs = jnp.where(jax.random.randint(sign_key, (RANK, 1), 0, 2) == 0, -1.0, 1.0).astype(jnp.float32)
    strength = jax.random.uniform(strength_key, (RANK, 1), jnp.float32, 0.8, 1.6)
    shared = jnp.clip(jax.random.normal(shared_key, (1, CELLS), jnp.float32), -3.0, 3.0)
    own = 0.05 * jnp.clip(jax.random.normal(own_key, (RANK, CELLS), jnp.float32), -6.0, 6.0)
    return (signs * strength * shared + own).astype(jnp.bfloat16)


def level_of(key, extent, pieces, low, largest):
    def one(dim, parts):
        heights = jax.random.uniform(jax.random.fold_in(jax.random.fold_in(key, 6), dim), (parts,), jnp.float32, low / len(pieces), largest / len(pieces))
        return jnp.repeat(jnp.exp(heights), extent[dim] // parts).reshape((-1,) + (1,) * (len(extent) - dim - 1))

    gain = one(*pieces[0])
    for cut in pieces[1:]:
        gain = gain * one(*cut)
    return gain


def centred(key, extent, spread, most, split=(), kind=jnp.bfloat16):
    result = jax.random.normal(key, extent, jnp.float32) * spread
    if len(split) > 0:
        result = level_of(key, extent, split, -0.22, 0.18) * result
    return jnp.clip(result, min=-most, max=most).astype(kind)


def setup_inputs(seed: int = 0) -> dict:
    keys = jax.random.split(jax.random.key(seed), 6)
    series = centred(keys[0], (DAYS, CELLS), 1.0, 6.0, ((1, 32),))
    lag_weight = jnp.clip(jnp.exp(jax.random.uniform(keys[1], (LAGS,), jnp.float32, math.log(0.25), math.log(1.0))), 0.25, 1.0)
    start_basis = draw_start_basis(jax.random.fold_in(keys[5], 71), 0)
    block_pairs = draw_block_pairs(jax.random.fold_in(keys[5], 71), 0)
    pair_count = draw_pair_count(jax.random.fold_in(keys[5], 71), 0)
    return {"series": series, "lag_weight": lag_weight, "start_basis": start_basis, "block_pairs": block_pairs, "pair_count": pair_count}


BETA_CORR = 8.0
GRAM_EPS = 1e-05
HIGHEST = lax.Precision.HIGHEST

def lagged_tile(lead_block, trail_block, lag_weight, tile_scale):
    day_count = lead_block.shape[0]
    block_width = lead_block.shape[1]
    lag_count = lag_weight.shape[0]
    zero_rows = jnp.zeros((lag_count, block_width), lead_block.dtype)
    lead_padded = jnp.concatenate([lead_block, zero_rows], axis=0)
    trail_padded = jnp.concatenate([trail_block, zero_rows], axis=0)
    lead_shifted = jnp.concatenate([lead_padded[offset:offset + day_count] for offset in range(lag_count)], axis=1)
    trail_shifted = jnp.concatenate([trail_padded[offset:offset + day_count] for offset in range(lag_count)], axis=1)
    contract = (((0,), (0,)), ((), ()))
    forward = lax.dot_general(lead_shifted, trail_block, contract, precision=HIGHEST)
    backward = lax.dot_general(lead_block, trail_shifted, contract, precision=HIGHEST)
    forward = forward.reshape(lag_count, block_width, block_width)
    backward = jnp.transpose(backward.reshape(block_width, lag_count, block_width), (1, 0, 2))
    soft_corr = jnp.tanh(BETA_CORR / day_count * (forward + backward))
    weighted = lax.optimization_barrier(jnp.sum(lag_weight[:, None, None] * soft_corr, axis=0))
    return (tile_scale * weighted).astype(jnp.bfloat16)

def network_product(basis_bf, series_full, lag_weight, block_pairs, pair_count):
    basis_full = basis_bf.astype(jnp.float32)
    slot_total = block_pairs.shape[2]
    lead_ids = block_pairs[:, :, :, 0].reshape(-1).astype(jnp.int32)
    trail_ids = block_pairs[:, :, :, 1].reshape(-1).astype(jnp.int32)
    alive = (jnp.arange(slot_total, dtype=jnp.int32)[None, :] < pair_count.reshape(-1, 1)).reshape(-1)
    tile_scale = 0.25 / math.sqrt(BLOCK)

    def one_slot(product, item):
        lead_id, trail_id, slot_alive = item
        lead_start = (lead_id * BLOCK).astype(jnp.int32)
        trail_start = (trail_id * BLOCK).astype(jnp.int32)

        def added(total):
            lead_block = lax.dynamic_slice_in_dim(series_full, lead_start, BLOCK, 1)
            trail_block = lax.dynamic_slice_in_dim(series_full, trail_start, BLOCK, 1)
            tile = lagged_tile(lead_block, trail_block, lag_weight, tile_scale).astype(jnp.float32)
            lead_basis = lax.dynamic_slice_in_dim(basis_full, lead_start, BLOCK, 1)
            trail_basis = lax.dynamic_slice_in_dim(basis_full, trail_start, BLOCK, 1)
            into_rows = jnp.dot(trail_basis, tile.T, precision=HIGHEST)
            into_cols = jnp.dot(lead_basis, tile, precision=HIGHEST)
            current = lax.dynamic_slice_in_dim(total, lead_start, BLOCK, 1)
            total = lax.dynamic_update_slice_in_dim(total, current + into_rows, lead_start, 1)
            current = lax.dynamic_slice_in_dim(total, trail_start, BLOCK, 1)
            return lax.dynamic_update_slice_in_dim(total, current + into_cols, trail_start, 1)
        return (lax.cond(slot_alive, added, lambda total: total, product), None)
    initial = jnp.zeros((RANK, CELLS), jnp.float32)
    product, ignored = lax.scan(one_slot, initial, (lead_ids, trail_ids, alive))
    return product

def orthonormal(product):
    gram = jnp.dot(product, product.T, precision=HIGHEST) / CELLS + GRAM_EPS * jnp.eye(RANK, dtype=jnp.float32)
    lower = jnp.linalg.cholesky(gram)
    return lax.linalg.triangular_solve(lower, product, left_side=True, lower=True)

def reference(series, lag_weight, start_basis, block_pairs, pair_count):
    series_full = series.astype(jnp.float32)
    current = start_basis
    basis = start_basis.astype(jnp.float32)
    for iteration in range(ITERS):
        product = network_product(current, series_full, lag_weight, block_pairs, pair_count)
        basis = orthonormal(product)
        current = basis.astype(jnp.bfloat16)
    final = network_product(current, series_full, lag_weight, block_pairs, pair_count)
    rayleigh = jnp.dot(final, current.astype(jnp.float32).T, precision=HIGHEST) / CELLS
    return (basis, rayleigh)
```

```python
import math

import jax
import jax.numpy as jnp
from jax import lax
from jax.experimental import pallas as pl
from jax.experimental.pallas import tpu as pltpu
from jax.sharding import PartitionSpec as P

BLOCK = 256
ITERS = 2


BETA_CORR = 8.0
GRAM_EPS = 1e-05
HIGHEST = lax.Precision.HIGHEST


def lagged_tile(lead_block, trail_block, lag_weight, tile_scale):
    day_count = lead_block.shape[0]
    block_width = lead_block.shape[1]
    lag_count = lag_weight.shape[0]
    zero_rows = jnp.zeros((lag_count, block_width), lead_block.dtype)
    lead_padded = jnp.concatenate([lead_block, zero_rows], axis=0)
    trail_padded = jnp.concatenate([trail_block, zero_rows], axis=0)
    lead_shifted = jnp.concatenate(
        [lead_padded[offset : offset + day_count] for offset in range(lag_count)], axis=1
    )
    trail_shifted = jnp.concatenate(
        [trail_padded[offset : offset + day_count] for offset in range(lag_count)], axis=1
    )
    contract = (((0,), (0,)), ((), ()))
    forward = lax.dot_general(
        lead_shifted, trail_block, contract, preferred_element_type=jnp.float32
    )
    backward = lax.dot_general(
        lead_block, trail_shifted, contract, preferred_element_type=jnp.float32
    )
    forward = forward.reshape(lag_count, block_width, block_width)
    backward = jnp.transpose(backward.reshape(block_width, lag_count, block_width), (1, 0, 2))
    soft_corr = jnp.tanh(BETA_CORR / day_count * (forward + backward))
    weighted = jnp.sum(lag_weight[:, None, None] * soft_corr, axis=0)
    return (tile_scale * weighted).astype(jnp.bfloat16)


def local(series, lag_weight, start_basis, block_pairs, pair_count):
    n_rows = lax.axis_size("row")
    n_cols = lax.axis_size("col")
    row_index = lax.axis_index("row")
    local_cells = series.shape[1]
    local_blocks = local_cells // BLOCK
    row_blocks = local_blocks * n_cols
    col_blocks = local_blocks * n_rows
    slot_total = block_pairs.shape[2]
    cell_total = local_cells * n_rows * n_cols
    rank_size = start_basis.shape[0]
    tile_scale = 0.25 / math.sqrt(BLOCK)
    row_series = lax.all_gather(series, "col", axis=1, tiled=True)
    col_series = lax.all_gather(series, "row", axis=1, tiled=True)
    slot_pairs = block_pairs.reshape(slot_total, 2)
    slot_count = pair_count.reshape(1)
    row_first = row_index * row_blocks
    slot_ids = jnp.arange(slot_total, dtype=jnp.int32)
    own_rows = slot_pairs[:, 0] - row_first
    global_block = slot_pairs[:, 1]
    own_cols = global_block // local_blocks // n_cols * local_blocks + global_block % local_blocks
    built_count = slot_count[0]
    tile_rows = own_rows
    tile_cols = own_cols
    tile_rows = jnp.clip(tile_rows, 0, row_blocks - 1)
    tile_cols = jnp.clip(tile_cols, 0, col_blocks - 1)
    live_slots = slot_ids < built_count

    def build_one(slot, tiles):
        lead_block = lax.dynamic_slice_in_dim(row_series, tile_rows[slot] * BLOCK, BLOCK, 1)
        trail_block = lax.dynamic_slice_in_dim(col_series, tile_cols[slot] * BLOCK, BLOCK, 1)
        tile = lagged_tile(lead_block, trail_block, lag_weight, tile_scale)
        return lax.dynamic_update_index_in_dim(tiles, tile, slot, 0)

    tiles = lax.fori_loop(
        0, built_count, build_one, jnp.zeros((slot_total, BLOCK, BLOCK), jnp.bfloat16)
    )
    live_float = live_slots.astype(jnp.float32)[:, None]
    row_onehot = (tile_rows[:, None] == jnp.arange(row_blocks, dtype=jnp.int32)[None, :]).astype(
        jnp.float32
    ) * live_float
    col_onehot = (tile_cols[:, None] == jnp.arange(col_blocks, dtype=jnp.int32)[None, :]).astype(
        jnp.float32
    ) * live_float

    def project(basis_now):
        row_basis = lax.all_gather(basis_now, "col", axis=1, tiled=True).reshape(
            rank_size, row_blocks, BLOCK
        )
        col_basis = lax.all_gather(basis_now, "row", axis=1, tiled=True)
        col_basis = col_basis.reshape(rank_size, col_blocks, BLOCK)
        lead_basis = jnp.take(row_basis, tile_rows, axis=1)
        trail_basis = jnp.take(col_basis, tile_cols, axis=1)
        into_cols = jnp.einsum(
            "ksa,sab->ksb", lead_basis, tiles, preferred_element_type=jnp.float32
        )
        return (trail_basis, into_cols)

    current = start_basis
    basis = start_basis.astype(jnp.float32)
    for iteration in range(ITERS):
        network_trail_basis, network_into_cols = project(current)
        into_rows = jnp.einsum(
            "ksb,sab->ksa", network_trail_basis, tiles, preferred_element_type=jnp.float32
        )
        row_part = jnp.einsum("ksa,sr->kra", into_rows, row_onehot, precision=HIGHEST)
        row_part = row_part.reshape(rank_size, row_blocks * BLOCK)
        col_part = jnp.einsum("ksb,sr->krb", network_into_cols, col_onehot, precision=HIGHEST)
        col_part = col_part.reshape(rank_size, col_blocks * BLOCK)
        row_total = lax.psum_scatter(row_part, "col", scatter_dimension=1, tiled=True)
        col_total = lax.psum_scatter(col_part, "row", scatter_dimension=1, tiled=True)
        product = row_total + col_total
        local_gram = jnp.dot(product, product.T, precision=HIGHEST)
        gram = lax.psum(local_gram, ("row", "col")) / cell_total
        gram = gram + GRAM_EPS * jnp.eye(rank_size, dtype=jnp.float32)
        lower = jnp.linalg.cholesky(gram)
        basis = lax.linalg.triangular_solve(lower, product, left_side=True, lower=True)
        current = basis.astype(jnp.bfloat16)
    trail_basis, into_cols = project(current)
    masked_cols = into_cols * live_float[None, :, :]
    local_form = jnp.einsum(
        "ksb,lsb->kl", masked_cols, trail_basis.astype(jnp.float32), precision=HIGHEST
    )
    local_form = local_form + local_form.T
    rayleigh = lax.psum(local_form, ("row", "col")) / cell_total
    return (basis, rayleigh)


VMEM_BYTES = 48 * 2**20
MESH = pl.DeviceIdType.MESH
NT = (((1,), (1,)), ((), ()))


def pack(square):
    quarter = square.shape[0] // 4
    return jnp.concatenate([square[i * quarter : (i + 1) * quarter] for i in range(4)], axis=1)


def unpack(packed):
    width = packed.shape[1] // 4
    return jnp.concatenate([packed[:, i * width : (i + 1) * width] for i in range(4)], axis=0)


def inverse_factor(gram):
    size = gram.shape[0]
    rows = lax.broadcasted_iota(jnp.int32, (size, size), 0)
    lanes = lax.broadcasted_iota(jnp.int32, (size, size), 1)
    both = jnp.concatenate([gram, (rows == lanes).astype(jnp.float32)], axis=1)
    groups = [both[i : i + 8] for i in range(0, size, 8)]
    row_ids = lax.broadcasted_iota(jnp.int32, (8, 1), 0)
    for k in range(size):
        home = k // 8
        pivot_row = groups[home][k % 8 : k % 8 + 1]
        scaled_row = pivot_row * (1.0 / pivot_row[:, k : k + 1])
        for g in range(home, len(groups)):
            column = groups[g][:, k : k + 1]
            if g == home:
                column = jnp.where(row_ids > k % 8, column, 0.0)
            groups[g] = groups[g] - column * scaled_row
    both = jnp.concatenate(groups, axis=0)
    pivots = jnp.sum(jnp.where(rows == lanes, both[:, :size], 0.0), axis=1, keepdims=True)
    return both[:, size:] / jnp.sqrt(pivots)


def kernel(
    n_rows, n_cols, days, rank, lags,
    own_ref, weight_ref, basis_ref, rayleigh_ref,
    held, tiles, stack, dots, parts, forms, counts, send_sem, recv_sem,
):
    n_blocks = n_rows * n_cols
    depth = n_cols // 2
    half = n_blocks // 2
    width = own_ref.shape[1]
    chunk = width // 2
    cells = n_blocks * width
    tile_scale = 0.25 / math.sqrt(width)
    row, col = lax.axis_index("row"), lax.axis_index("col")
    x, core = row // 2, lax.rem(row, 2)
    z, y = col // 2, lax.rem(col, 2)
    me = row * n_cols + col

    def place(flip_a, flip_b, other, far):
        side = lax.rem(core + other, 2)
        flip_x = flip_a * (1 - side) + flip_b * side
        flip_y = flip_b * (1 - side) + flip_a * side
        at_x, at_y = lax.rem(x + flip_x, 2), lax.rem(y + flip_y, 2)
        at_z = lax.rem(z + far, depth)
        return at_x * 2 + side, at_z * 2 + at_y

    def block_of(s):
        at_row, at_col = place(
            lax.rem(s // depth, 2), lax.rem(s // (2 * depth), 2), s // half, lax.rem(s, depth)
        )
        return at_row * n_cols + at_col

    peer_a = (lax.rem(x + 1 - core, 2) * 2 + core, z * 2 + lax.rem(y + core, 2))
    peer_b = (lax.rem(x + core, 2) * 2 + core, z * 2 + lax.rem(y + 1 - core, 2))
    sibling = (x * 2 + 1 - core, col)
    line = [(row, lax.rem(z + far, depth) * 2 + y) for far in range(1, depth)]

    barrier = pltpu.get_barrier_semaphore()
    for peer in line + [peer_a, peer_b, sibling]:
        pl.semaphore_signal(barrier, inc=1, device_id=peer, device_id_type=MESH)
    own = own_ref[...]
    held[me] = own
    pl.semaphore_wait(barrier, len(line) + 3)

    first_a, first_b, first_s = depth - 1, 2 * depth - 1, 4 * depth - 1

    def copy(step, buffer, block, send, recv, peer):
        return pltpu.make_async_remote_copy(
            src_ref=buffer.at[block],
            dst_ref=buffer.at[block],
            send_sem=send_sem.at[step, send],
            recv_sem=recv_sem.at[step, recv],
            device_id=peer,
            device_id_type=MESH,
        )

    def forward(step, buffer, k):
        block = block_of(k)

        @pl.when(k < depth)
        def _():
            copy(step, buffer, block, first_a + k, depth + k, peer_a).start()

        @pl.when(k < 2 * depth)
        def _():
            copy(step, buffer, block, first_b + k, 2 * depth + k, peer_b).start()

        copy(step, buffer, block, first_s + k, half + k, sibling).start()

    def begin(step, buffer):
        for far in range(1, depth):
            copy(step, buffer, me, far - 1, depth - far, line[far - 1]).start()
        forward(step, buffer, 0)

    def arrive(step, buffer, s):
        copy(step, buffer, block_of(s), 0, s, sibling).wait_recv()

    def gather(step, buffer, use, carry):
        carry = use(me, carry)
        arrive(step, buffer, half)
        carry = use(block_of(half), carry)

        def body(k, carry):
            arrive(step, buffer, k)
            forward(step, buffer, k)
            carry = use(block_of(k), carry)
            arrive(step, buffer, half + k)
            return use(block_of(half + k), carry)

        return lax.fori_loop(1, half, body, carry)

    begin(0, held)
    lanes = lax.broadcasted_iota(jnp.int32, (width, days), 1)
    turned = own[:days].astype(jnp.float32).T
    shifted = [turned]
    for lag in range(1, lags):
        shifted.append(jnp.where(lanes < days - lag, pltpu.roll(turned, days - lag, 1), 0.0))
        shifted.append(jnp.where(lanes >= lag, pltpu.roll(turned, lag, 1), 0.0))
    shifts = len(shifted)
    for i, part in enumerate(shifted):
        for q in range(2):
            stack[q, i * chunk : (i + 1) * chunk, :] = part[q * chunk : (q + 1) * chunk].astype(
                jnp.bfloat16
            )
    weights = [weight_ref[lag] for lag in range(lags)]

    def build(block, carry):
        series = held[block, 0:days, :]
        for q in range(2):
            sums = jnp.dot(stack[q], series, preferred_element_type=jnp.float32)
            rows = [sums[i * chunk : (i + 1) * chunk] for i in range(shifts)]
            total = weights[0] * jnp.tanh(2 * BETA_CORR / days * rows[0])
            for lag in range(1, lags):
                total += weights[lag] * jnp.tanh(
                    BETA_CORR / days * (rows[2 * lag - 1] + rows[2 * lag])
                )
            tiles[block, q * chunk : (q + 1) * chunk, :] = (tile_scale * total).astype(
                jnp.bfloat16
            )
        dots[block] = lax.dot_general(
            held[block, days : days + rank, :], tiles[block], NT, preferred_element_type=jnp.float32
        )
        return carry

    gather(0, held, build, jnp.int32(0))

    count_rows = counts.shape[0]

    def add_counts(block, total):
        return total + held[block, days + rank : days + rank + count_rows, :].astype(jnp.float32)

    zero_counts = jnp.zeros((count_rows, width), jnp.float32)
    total = lax.fori_loop(0, n_blocks, add_counts, zero_counts)
    count_lanes = lax.broadcasted_iota(jnp.int32, (count_rows, width), 1)
    mine = jnp.sum(jnp.where(count_lanes == me, total, 0.0), axis=1, keepdims=True)
    counts[...] = jnp.broadcast_to(mine, (count_rows, width))

    zero = jnp.zeros((rank, width), jnp.float32)
    product = lax.fori_loop(
        0, n_blocks, lambda b, acc: acc + counts[pl.ds(b, 1), :] * dots[b], zero
    )

    inverse = None
    for step in range(ITERS):
        buffer = parts.at[step]
        buffer[me, 0:rank, :] = product
        local_gram = lax.dot_general(
            product, product, NT, precision=HIGHEST, preferred_element_type=jnp.float32
        )
        buffer[me, rank : rank + rank // 4, :] = pack(local_gram)
        begin(step + 1, buffer)

        def multiply(block, acc):
            part = buffer[block, 0:rank, :]
            high = part.astype(jnp.bfloat16)
            rest = part - high.astype(jnp.float32)
            middle = rest.astype(jnp.bfloat16)
            low = (rest - middle.astype(jnp.float32)).astype(jnp.bfloat16)
            split = jnp.concatenate([high, middle, low], axis=0)
            out = lax.dot_general(split, tiles[block], NT, preferred_element_type=jnp.float32)
            out = out[:rank] + (out[rank : 2 * rank] + out[2 * rank :])
            return acc + counts[pl.ds(block, 1), :] * out

        onward = gather(step + 1, buffer, multiply, zero)

        if step == ITERS - 1:
            local_form = lax.dot_general(
                onward, product, NT, precision=HIGHEST, preferred_element_type=jnp.float32
            )
            forms[me] = pack(local_form)
            begin(ITERS + 1, forms)

        zero_packed = jnp.zeros((rank // 4, width), jnp.float32)
        packed = lax.fori_loop(
            0,
            n_blocks,
            lambda b, acc: acc + buffer[b, rank : rank + rank // 4, :],
            zero_packed,
        )
        eye_rows = lax.broadcasted_iota(jnp.int32, (rank, rank), 0)
        eye_lanes = lax.broadcasted_iota(jnp.int32, (rank, rank), 1)
        eye = (eye_rows == eye_lanes).astype(jnp.float32)
        inverse = inverse_factor(unpack(packed) / cells + GRAM_EPS * eye)
        if step == ITERS - 1:
            basis_ref[...] = jnp.dot(
                inverse, product, precision=HIGHEST, preferred_element_type=jnp.float32
            )
        else:
            product = jnp.dot(
                inverse, onward, precision=HIGHEST, preferred_element_type=jnp.float32
            )

    gather(ITERS + 1, forms, lambda block, carry: carry, jnp.int32(0))
    packed = lax.fori_loop(0, n_blocks, lambda b, acc: acc + forms[b], zero_packed)
    left = jnp.dot(
        inverse, unpack(packed), precision=HIGHEST, preferred_element_type=jnp.float32
    )
    rayleigh_ref[...] = (
        lax.dot_general(left, inverse, NT, precision=HIGHEST, preferred_element_type=jnp.float32)
        / cells
    )

    for step in range(ITERS + 2):
        buffer = held if step == 0 else forms if step == ITERS + 1 else parts.at[step - 1]

        def drain(i, carry):
            copy(step, buffer, me, i, 0, sibling).wait_send()
            return carry

        lax.fori_loop(0, n_blocks - 1, drain, jnp.int32(0))


def sizes(mesh_rows, mesh_cols, series, start_basis):
    n_blocks = mesh_rows * mesh_cols
    days, width = series
    rank = start_basis[0]
    count_rows = -(-n_blocks // 16) * 16
    return n_blocks, days, width, rank, count_rows, days + rank + count_rows


def scratch(mesh_rows, mesh_cols, series, start_basis, lags):
    n_blocks, days, width, rank, count_rows, held_rows = sizes(
        mesh_rows, mesh_cols, series, start_basis
    )
    return [
        ((n_blocks, held_rows, width), jnp.bfloat16),
        ((n_blocks, width, width), jnp.bfloat16),
        ((2, (2 * lags - 1) * width // 2, days), jnp.bfloat16),
        ((n_blocks, rank, width), jnp.float32),
        ((ITERS, n_blocks, rank + rank // 4, width), jnp.float32),
        ((n_blocks, rank // 4, width), jnp.float32),
        ((count_rows, width), jnp.float32),
    ]


def fused(series, lag_weight, start_basis, block_pairs, pair_count):
    n_rows, n_cols = lax.axis_size("row"), lax.axis_size("col")
    n_blocks, days, width, rank, count_rows, held_rows = sizes(
        n_rows, n_cols, series.shape, start_basis.shape
    )
    slot_total = block_pairs.shape[2]
    slot_pairs = block_pairs.reshape(slot_total, 2)
    live = (jnp.arange(slot_total, dtype=jnp.int32) < pair_count.reshape(1)[0])[:, None]
    ids = jnp.arange(n_blocks, dtype=jnp.int32)[None, :]
    leads = ((slot_pairs[:, :1] == ids) & live).astype(jnp.bfloat16)
    trails = (slot_pairs[:, 1:] == ids).astype(jnp.bfloat16)
    first = lax.dot_general(
        jnp.concatenate([leads, trails * live.astype(jnp.bfloat16)], axis=0),
        jnp.concatenate([trails, leads], axis=0),
        (((0,), (0,)), ((), ())),
        preferred_element_type=jnp.float32,
    )
    pair_counts = jnp.pad(
        first.astype(jnp.bfloat16), ((0, count_rows - n_blocks), (0, width - n_blocks))
    )
    own = jnp.concatenate([series, start_basis, pair_counts], axis=0)
    lags = lag_weight.shape[0]
    shapes = scratch(n_rows, n_cols, series.shape, start_basis.shape, lags)

    def body(*refs):
        kernel(n_rows, n_cols, days, rank, lags, *refs)

    return pl.pallas_call(
        body,
        out_shape=(
            jax.ShapeDtypeStruct((rank, width), jnp.float32),
            jax.ShapeDtypeStruct((rank, rank), jnp.float32),
        ),
        in_specs=[
            pl.BlockSpec(memory_space=pltpu.VMEM),
            pl.BlockSpec(memory_space=pltpu.SMEM),
        ],
        out_specs=(
            pl.BlockSpec(memory_space=pltpu.VMEM),
            pl.BlockSpec(memory_space=pltpu.VMEM),
        ),
        scratch_shapes=[pltpu.VMEM(shape, kind) for shape, kind in shapes]
        + [
            pltpu.SemaphoreType.DMA((ITERS + 2, n_blocks - 1)),
            pltpu.SemaphoreType.DMA((ITERS + 2, n_blocks)),
        ],
        compiler_params=pltpu.CompilerParams(
            collective_id=0, has_side_effects=True, vmem_limit_bytes=VMEM_BYTES
        ),
        name="subspace",
    )(own, lag_weight)


def either(n_rows, n_cols):
    def run(series, lag_weight, start_basis, block_pairs, pair_count):
        shapes = scratch(n_rows, n_cols, series.shape, start_basis.shape, lag_weight.shape[0])
        held_bytes = sum(math.prod(s) * jnp.dtype(kind).itemsize for s, kind in shapes)
        fits = held_bytes <= VMEM_BYTES * 3 // 4
        one_block = series.shape[1] == BLOCK and n_rows * n_cols <= BLOCK
        if fits and one_block and n_rows == 2 * 2 and n_cols % 2 == 0:
            return fused(series, lag_weight, start_basis, block_pairs, pair_count)
        return local(series, lag_weight, start_basis, block_pairs, pair_count)

    return run


def solution(mesh):
    return jax.shard_map(
        either(mesh.shape["row"], mesh.shape["col"]),
        mesh=mesh,
        in_specs=(
            P(None, ("row", "col")),
            P(),
            P(None, ("row", "col")),
            P("row", "col", None, None),
            P("row", "col"),
        ),
        out_specs=(P(None, ("row", "col")), P()),
        check_vma=False,
    )
```

```python
import math

import jax
import jax.numpy as jnp
from jax import lax
from jax.experimental import pallas as pl
from jax.experimental.pallas import tpu as pltpu
from jax.sharding import PartitionSpec as P

BLOCK = 256
ITERS = 2


BETA_CORR = 8.0
GRAM_EPS = 1e-05
HIGHEST = lax.Precision.HIGHEST


def lagged_tile(lead_block, trail_block, lag_weight, tile_scale):
    day_count = lead_block.shape[0]
    block_width = lead_block.shape[1]
    lag_count = lag_weight.shape[0]
    zero_rows = jnp.zeros((lag_count, block_width), lead_block.dtype)
    lead_padded = jnp.concatenate([lead_block, zero_rows], axis=0)
    trail_padded = jnp.concatenate([trail_block, zero_rows], axis=0)
    lead_shifted = jnp.concatenate(
        [lead_padded[offset : offset + day_count] for offset in range(lag_count)], axis=1
    )
    trail_shifted = jnp.concatenate(
        [trail_padded[offset : offset + day_count] for offset in range(lag_count)], axis=1
    )
    contract = (((0,), (0,)), ((), ()))
    forward = lax.dot_general(
        lead_shifted, trail_block, contract, preferred_element_type=jnp.float32
    )
    backward = lax.dot_general(
        lead_block, trail_shifted, contract, preferred_element_type=jnp.float32
    )
    forward = forward.reshape(lag_count, block_width, block_width)
    backward = jnp.transpose(backward.reshape(block_width, lag_count, block_width), (1, 0, 2))
    soft_corr = jnp.tanh(BETA_CORR / day_count * (forward + backward))
    weighted = jnp.sum(lag_weight[:, None, None] * soft_corr, axis=0)
    return (tile_scale * weighted).astype(jnp.bfloat16)


def local(series, lag_weight, start_basis, block_pairs, pair_count):
    n_rows = lax.axis_size("row")
    n_cols = lax.axis_size("col")
    row_index = lax.axis_index("row")
    local_cells = series.shape[1]
    local_blocks = local_cells // BLOCK
    row_blocks = local_blocks * n_cols
    col_blocks = local_blocks * n_rows
    slot_total = block_pairs.shape[2]
    cell_total = local_cells * n_rows * n_cols
    rank_size = start_basis.shape[0]
    tile_scale = 0.25 / math.sqrt(BLOCK)
    row_series = lax.all_gather(series, "col", axis=1, tiled=True)
    col_series = lax.all_gather(series, "row", axis=1, tiled=True)
    slot_pairs = block_pairs.reshape(slot_total, 2)
    slot_count = pair_count.reshape(1)
    row_first = row_index * row_blocks
    slot_ids = jnp.arange(slot_total, dtype=jnp.int32)
    own_rows = slot_pairs[:, 0] - row_first
    global_block = slot_pairs[:, 1]
    own_cols = global_block // local_blocks // n_cols * local_blocks + global_block % local_blocks
    built_count = slot_count[0]
    tile_rows = own_rows
    tile_cols = own_cols
    tile_rows = jnp.clip(tile_rows, 0, row_blocks - 1)
    tile_cols = jnp.clip(tile_cols, 0, col_blocks - 1)
    live_slots = slot_ids < built_count

    def build_one(slot, tiles):
        lead_block = lax.dynamic_slice_in_dim(row_series, tile_rows[slot] * BLOCK, BLOCK, 1)
        trail_block = lax.dynamic_slice_in_dim(col_series, tile_cols[slot] * BLOCK, BLOCK, 1)
        tile = lagged_tile(lead_block, trail_block, lag_weight, tile_scale)
        return lax.dynamic_update_index_in_dim(tiles, tile, slot, 0)

    tiles = lax.fori_loop(
        0, built_count, build_one, jnp.zeros((slot_total, BLOCK, BLOCK), jnp.bfloat16)
    )
    live_float = live_slots.astype(jnp.float32)[:, None]
    row_onehot = (tile_rows[:, None] == jnp.arange(row_blocks, dtype=jnp.int32)[None, :]).astype(
        jnp.float32
    ) * live_float
    col_onehot = (tile_cols[:, None] == jnp.arange(col_blocks, dtype=jnp.int32)[None, :]).astype(
        jnp.float32
    ) * live_float

    def project(basis_now):
        row_basis = lax.all_gather(basis_now, "col", axis=1, tiled=True).reshape(
            rank_size, row_blocks, BLOCK
        )
        col_basis = lax.all_gather(basis_now, "row", axis=1, tiled=True)
        col_basis = col_basis.reshape(rank_size, col_blocks, BLOCK)
        lead_basis = jnp.take(row_basis, tile_rows, axis=1)
        trail_basis = jnp.take(col_basis, tile_cols, axis=1)
        into_cols = jnp.einsum(
            "ksa,sab->ksb", lead_basis, tiles, preferred_element_type=jnp.float32
        )
        return (trail_basis, into_cols)

    current = start_basis
    basis = start_basis.astype(jnp.float32)
    for iteration in range(ITERS):
        network_trail_basis, network_into_cols = project(current)
        into_rows = jnp.einsum(
            "ksb,sab->ksa", network_trail_basis, tiles, preferred_element_type=jnp.float32
        )
        row_part = jnp.einsum("ksa,sr->kra", into_rows, row_onehot, precision=HIGHEST)
        row_part = row_part.reshape(rank_size, row_blocks * BLOCK)
        col_part = jnp.einsum("ksb,sr->krb", network_into_cols, col_onehot, precision=HIGHEST)
        col_part = col_part.reshape(rank_size, col_blocks * BLOCK)
        row_total = lax.psum_scatter(row_part, "col", scatter_dimension=1, tiled=True)
        col_total = lax.psum_scatter(col_part, "row", scatter_dimension=1, tiled=True)
        product = row_total + col_total
        local_gram = jnp.dot(product, product.T, precision=HIGHEST)
        gram = lax.psum(local_gram, ("row", "col")) / cell_total
        gram = gram + GRAM_EPS * jnp.eye(rank_size, dtype=jnp.float32)
        lower = jnp.linalg.cholesky(gram)
        basis = lax.linalg.triangular_solve(lower, product, left_side=True, lower=True)
        current = basis.astype(jnp.bfloat16)
    trail_basis, into_cols = project(current)
    masked_cols = into_cols * live_float[None, :, :]
    local_form = jnp.einsum(
        "ksb,lsb->kl", masked_cols, trail_basis.astype(jnp.float32), precision=HIGHEST
    )
    local_form = local_form + local_form.T
    rayleigh = lax.psum(local_form, ("row", "col")) / cell_total
    return (basis, rayleigh)


VMEM_BYTES = 48 * 2**20
MESH = pl.DeviceIdType.MESH
NT = (((1,), (1,)), ((), ()))


def pack(square):
    quarter = square.shape[0] // 4
    return jnp.concatenate([square[i * quarter : (i + 1) * quarter] for i in range(4)], axis=1)


def unpack(packed):
    width = packed.shape[1] // 4
    return jnp.concatenate([packed[:, i * width : (i + 1) * width] for i in range(4)], axis=0)


def inverse_factor(gram):
    size = gram.shape[0]
    rows = lax.broadcasted_iota(jnp.int32, (size, size), 0)
    lanes = lax.broadcasted_iota(jnp.int32, (size, size), 1)
    both = jnp.concatenate([gram, (rows == lanes).astype(jnp.float32)], axis=1)
    groups = [both[i : i + 8] for i in range(0, size, 8)]
    row_ids = lax.broadcasted_iota(jnp.int32, (8, 1), 0)
    for k in range(size):
        home = k // 8
        pivot_row = groups[home][k % 8 : k % 8 + 1]
        scaled_row = pivot_row * (1.0 / pivot_row[:, k : k + 1])
        for g in range(home, len(groups)):
            column = groups[g][:, k : k + 1]
            if g == home:
                column = jnp.where(row_ids > k % 8, column, 0.0)
            groups[g] = groups[g] - column * scaled_row
    both = jnp.concatenate(groups, axis=0)
    pivots = jnp.sum(jnp.where(rows == lanes, both[:, :size], 0.0), axis=1, keepdims=True)
    return both[:, size:] / jnp.sqrt(pivots)


def kernel(
    n_rows, n_cols, days, rank, lags,
    own_ref, weight_ref, basis_ref, rayleigh_ref,
    held, tiles, stack, dots, parts, forms, counts, send_sem, recv_sem,
):
    n_blocks = n_rows * n_cols
    depth = n_cols // 2
    half = n_blocks // 2
    width = own_ref.shape[1]
    chunk = width // 2
    cells = n_blocks * width
    tile_scale = 0.25 / math.sqrt(width)
    row, col = lax.axis_index("row"), lax.axis_index("col")
    x, core = row // 2, lax.rem(row, 2)
    z, y = col // 2, lax.rem(col, 2)
    me = row * n_cols + col

    def place(flip_a, flip_b, other, far):
        side = lax.rem(core + other, 2)
        flip_x = flip_a * (1 - side) + flip_b * side
        flip_y = flip_b * (1 - side) + flip_a * side
        at_x, at_y = lax.rem(x + flip_x, 2), lax.rem(y + flip_y, 2)
        at_z = lax.rem(z + far, depth)
        return at_x * 2 + side, at_z * 2 + at_y

    def block_of(s):
        at_row, at_col = place(
            lax.rem(s // depth, 2), lax.rem(s // (2 * depth), 2), s // half, lax.rem(s, depth)
        )
        return at_row * n_cols + at_col

    peer_a = (lax.rem(x + 1 - core, 2) * 2 + core, z * 2 + lax.rem(y + core, 2))
    peer_b = (lax.rem(x + core, 2) * 2 + core, z * 2 + lax.rem(y + 1 - core, 2))
    sibling = (x * 2 + 1 - core, col)
    line = [(row, lax.rem(z + far, depth) * 2 + y) for far in range(1, depth)]

    barrier = pltpu.get_barrier_semaphore()
    for peer in line + [peer_a, peer_b, sibling]:
        pl.semaphore_signal(barrier, inc=1, device_id=peer, device_id_type=MESH)
    own = own_ref[...]
    held[me] = own
    pl.semaphore_wait(barrier, len(line) + 3)

    first_a, first_b, first_s = depth - 1, 2 * depth - 1, 4 * depth - 1

    def copy(step, buffer, block, send, recv, peer):
        return pltpu.make_async_remote_copy(
            src_ref=buffer.at[block],
            dst_ref=buffer.at[block],
            send_sem=send_sem.at[step, send],
            recv_sem=recv_sem.at[step, recv],
            device_id=peer,
            device_id_type=MESH,
        )

    def forward(step, buffer, k):
        block = block_of(k)

        @pl.when(k < depth)
        def _():
            copy(step, buffer, block, first_a + k, depth + k, peer_a).start()

        @pl.when(k < 2 * depth)
        def _():
            copy(step, buffer, block, first_b + k, 2 * depth + k, peer_b).start()

        copy(step, buffer, block, first_s + k, half + k, sibling).start()

    def begin(step, buffer):
        for far in range(1, depth):
            copy(step, buffer, me, far - 1, depth - far, line[far - 1]).start()
        forward(step, buffer, 0)

    def arrive(step, buffer, s):
        copy(step, buffer, block_of(s), 0, s, sibling).wait_recv()

    def gather(step, buffer, use, carry):
        carry = use(me, carry)
        arrive(step, buffer, half)
        carry = use(block_of(half), carry)

        def body(k, carry):
            arrive(step, buffer, k)
            forward(step, buffer, k)
            carry = use(block_of(k), carry)
            arrive(step, buffer, half + k)
            return use(block_of(half + k), carry)

        return lax.fori_loop(1, half, body, carry)

    def gather_early(step, buffer, use, carry):
        def body(k, carry):
            arrive(step, buffer, k)
            forward(step, buffer, k)
            carry = use(block_of(k - 1), carry)
            arrive(step, buffer, half + k - 1)
            return use(block_of(half + k - 1), carry)

        carry = lax.fori_loop(1, half, body, carry)
        carry = use(block_of(half - 1), carry)
        arrive(step, buffer, 2 * half - 1)
        return use(block_of(2 * half - 1), carry)

    begin(0, held)
    lanes = lax.broadcasted_iota(jnp.int32, (width, days), 1)
    turned = own[:days].astype(jnp.float32).T
    shifted = [2.0 * turned]
    for lag in range(1, lags):
        later = jnp.where(lanes < days - lag, pltpu.roll(turned, days - lag, 1), 0.0)
        earlier = jnp.where(lanes >= lag, pltpu.roll(turned, lag, 1), 0.0)
        shifted.append(later + earlier)
    for i, part in enumerate(shifted):
        for q in range(2):
            stack[q, i * chunk : (i + 1) * chunk, :] = part[q * chunk : (q + 1) * chunk].astype(
                jnp.bfloat16
            )
    weights = [weight_ref[lag] for lag in range(lags)]

    def build(block, carry):
        series = held[block, 0:days, :]
        for q in range(2):
            sums = jnp.dot(stack[q], series, preferred_element_type=jnp.float32)
            soft = jnp.tanh(BETA_CORR / days * sums)
            total = weights[0] * soft[:chunk]
            for lag in range(1, lags):
                total += weights[lag] * soft[lag * chunk : (lag + 1) * chunk]
            tiles[block, q * chunk : (q + 1) * chunk, :] = (tile_scale * total).astype(
                jnp.bfloat16
            )
        dots[block] = lax.dot_general(
            held[block, days : days + rank, :], tiles[block], NT, preferred_element_type=jnp.float32
        )
        return carry

    gather(0, held, build, jnp.int32(0))

    count_rows = counts.shape[0]

    def add_counts(block, total):
        return total + held[block, days + rank : days + rank + count_rows, :].astype(jnp.float32)

    zero_counts = jnp.zeros((count_rows, width), jnp.float32)
    total = lax.fori_loop(0, n_blocks, add_counts, zero_counts)
    count_lanes = lax.broadcasted_iota(jnp.int32, (count_rows, width), 1)
    mine = jnp.sum(jnp.where(count_lanes == me, total, 0.0), axis=1, keepdims=True)
    counts[...] = jnp.broadcast_to(mine, (count_rows, width))

    zero = jnp.zeros((rank, width), jnp.float32)
    product = lax.fori_loop(
        0, n_blocks, lambda b, acc: acc + counts[pl.ds(b, 1), :] * dots[b], zero
    )

    inverse = None
    for step in range(ITERS):
        buffer = parts.at[step]
        buffer[me, 0:rank, :] = product
        local_gram = lax.dot_general(
            product, product, NT, precision=HIGHEST, preferred_element_type=jnp.float32
        )
        buffer[me, rank : rank + rank // 4, :] = pack(local_gram)
        begin(step + 1, buffer)

        def multiply(block, acc):
            part = buffer[block, 0:rank, :]
            high = part.astype(jnp.bfloat16)
            rest = part - high.astype(jnp.float32)
            middle = rest.astype(jnp.bfloat16)
            low = (rest - middle.astype(jnp.float32)).astype(jnp.bfloat16)
            split = jnp.concatenate([high, middle, low], axis=0)
            out = lax.dot_general(split, tiles[block], NT, preferred_element_type=jnp.float32)
            out = out[:rank] + (out[rank : 2 * rank] + out[2 * rank :])
            return acc + counts[pl.ds(block, 1), :] * out

        onward = gather_early(step + 1, buffer, multiply, zero)

        if step == ITERS - 1:
            local_form = lax.dot_general(
                onward, product, NT, precision=HIGHEST, preferred_element_type=jnp.float32
            )
            forms[me] = pack(local_form)
            begin(ITERS + 1, forms)

        zero_packed = jnp.zeros((rank // 4, width), jnp.float32)
        packed = lax.fori_loop(
            0,
            n_blocks,
            lambda b, acc: acc + buffer[b, rank : rank + rank // 4, :],
            zero_packed,
        )
        eye_rows = lax.broadcasted_iota(jnp.int32, (rank, rank), 0)
        eye_lanes = lax.broadcasted_iota(jnp.int32, (rank, rank), 1)
        eye = (eye_rows == eye_lanes).astype(jnp.float32)
        inverse = inverse_factor(unpack(packed) / cells + GRAM_EPS * eye)
        if step == ITERS - 1:
            basis_ref[...] = jnp.dot(
                inverse, product, precision=HIGHEST, preferred_element_type=jnp.float32
            )
        else:
            product = jnp.dot(
                inverse, onward, precision=HIGHEST, preferred_element_type=jnp.float32
            )

    gather_early(ITERS + 1, forms, lambda block, carry: carry, jnp.int32(0))
    packed = lax.fori_loop(0, n_blocks, lambda b, acc: acc + forms[b], zero_packed)
    left = jnp.dot(
        inverse, unpack(packed), precision=HIGHEST, preferred_element_type=jnp.float32
    )
    rayleigh_ref[...] = (
        lax.dot_general(left, inverse, NT, precision=HIGHEST, preferred_element_type=jnp.float32)
        / cells
    )

    for step in range(ITERS + 2):
        buffer = held if step == 0 else forms if step == ITERS + 1 else parts.at[step - 1]

        def drain(i, carry):
            copy(step, buffer, me, i, 0, sibling).wait_send()
            return carry

        lax.fori_loop(0, n_blocks - 1, drain, jnp.int32(0))


def sizes(mesh_rows, mesh_cols, series, start_basis):
    n_blocks = mesh_rows * mesh_cols
    days, width = series
    rank = start_basis[0]
    count_rows = -(-n_blocks // 16) * 16
    return n_blocks, days, width, rank, count_rows, days + rank + count_rows


def scratch(mesh_rows, mesh_cols, series, start_basis, lags):
    n_blocks, days, width, rank, count_rows, held_rows = sizes(
        mesh_rows, mesh_cols, series, start_basis
    )
    return [
        ((n_blocks, held_rows, width), jnp.bfloat16),
        ((n_blocks, width, width), jnp.bfloat16),
        ((2, lags * width // 2, days), jnp.bfloat16),
        ((n_blocks, rank, width), jnp.float32),
        ((ITERS, n_blocks, rank + rank // 4, width), jnp.float32),
        ((n_blocks, rank // 4, width), jnp.float32),
        ((count_rows, width), jnp.float32),
    ]


def fused(series, lag_weight, start_basis, block_pairs, pair_count):
    n_rows, n_cols = lax.axis_size("row"), lax.axis_size("col")
    n_blocks, days, width, rank, count_rows, held_rows = sizes(
        n_rows, n_cols, series.shape, start_basis.shape
    )
    slot_total = block_pairs.shape[2]
    slot_pairs = block_pairs.reshape(slot_total, 2)
    live = (jnp.arange(slot_total, dtype=jnp.int32) < pair_count.reshape(1)[0])[:, None]
    ids = jnp.arange(n_blocks, dtype=jnp.int32)[None, :]
    leads = ((slot_pairs[:, :1] == ids) & live).astype(jnp.bfloat16)
    trails = (slot_pairs[:, 1:] == ids).astype(jnp.bfloat16)
    first = lax.dot_general(
        jnp.concatenate([leads, trails * live.astype(jnp.bfloat16)], axis=0),
        jnp.concatenate([trails, leads], axis=0),
        (((0,), (0,)), ((), ())),
        preferred_element_type=jnp.float32,
    )
    pair_counts = jnp.pad(
        first.astype(jnp.bfloat16), ((0, count_rows - n_blocks), (0, width - n_blocks))
    )
    own = jnp.concatenate([series, start_basis, pair_counts], axis=0)
    lags = lag_weight.shape[0]
    shapes = scratch(n_rows, n_cols, series.shape, start_basis.shape, lags)

    def body(*refs):
        kernel(n_rows, n_cols, days, rank, lags, *refs)

    return pl.pallas_call(
        body,
        out_shape=(
            jax.ShapeDtypeStruct((rank, width), jnp.float32),
            jax.ShapeDtypeStruct((rank, rank), jnp.float32),
        ),
        in_specs=[
            pl.BlockSpec(memory_space=pltpu.VMEM),
            pl.BlockSpec(memory_space=pltpu.SMEM),
        ],
        out_specs=(
            pl.BlockSpec(memory_space=pltpu.VMEM),
            pl.BlockSpec(memory_space=pltpu.VMEM),
        ),
        scratch_shapes=[pltpu.VMEM(shape, kind) for shape, kind in shapes]
        + [
            pltpu.SemaphoreType.DMA((ITERS + 2, n_blocks - 1)),
            pltpu.SemaphoreType.DMA((ITERS + 2, n_blocks)),
        ],
        compiler_params=pltpu.CompilerParams(
            collective_id=0, has_side_effects=True, vmem_limit_bytes=VMEM_BYTES
        ),
        name="subspace",
    )(own, lag_weight)


def either(n_rows, n_cols):
    def run(series, lag_weight, start_basis, block_pairs, pair_count):
        shapes = scratch(n_rows, n_cols, series.shape, start_basis.shape, lag_weight.shape[0])
        held_bytes = sum(math.prod(s) * jnp.dtype(kind).itemsize for s, kind in shapes)
        fits = held_bytes <= VMEM_BYTES * 3 // 4
        one_block = series.shape[1] == BLOCK and n_rows * n_cols <= BLOCK
        if fits and one_block and n_rows == 2 * 2 and n_cols % 2 == 0:
            return fused(series, lag_weight, start_basis, block_pairs, pair_count)
        return local(series, lag_weight, start_basis, block_pairs, pair_count)

    return run


def solution(mesh):
    return jax.shard_map(
        either(mesh.shape["row"], mesh.shape["col"]),
        mesh=mesh,
        in_specs=(
            P(None, ("row", "col")),
            P(),
            P(None, ("row", "col")),
            P("row", "col", None, None),
            P("row", "col"),
        ),
        out_specs=(P(None, ("row", "col")), P()),
        check_vma=False,
    )
```
